32 devices in a mesh: prod: 8 (over z, y), hid: 4 (over x, core).
Axes of the slice: x: 2, y: 2, z: 4, core: 2. Of those that a mesh axis runs over, the one named last changes fastest.
Arguments:
- fingerprints: bfloat16 [8192, 16384], P('prod'), may hold values from 0 to 3
- w_first: bfloat16 [16384, 2048], P(None, 'hid'), may hold values from -0.046875 to 0.046875
- b_first: float32 [2048], P('hid'), may hold values from -4 to 4
- w_second: bfloat16 [2048, 1024], replicated, may hold values from -0.125 to 0.125
- b_second: float32 [1024], replicated, may hold values from -4 to 4
- w_third: float32 [1024], replicated, may hold values from -0.1875 to 0.1875
- synth_block: int32 [16384, 3], P('prod'), may hold values from 0 to 7
- synth_row: int32 [16384, 3], P('prod'), may hold values from 0 to 1023
- third_used: int32 [16384], P('prod'), may hold values 0 or 1
Outputs:
- score: float32 [16384], P(('prod', 'hid'))
The draws below stay inside these ranges and needn't reach their ends.
Inputs may be any that keep to these rules, and one draw needn't show every extreme that they name: `synth_row`: rows within a block.
All inputs are finite; a program needn't handle non-finite values. No bound on the sum of `third_used` on one device may be relied on, other than what follows from the above.
Results may differ from the reference program's by a relative error of at most 0.0083.
Values may be sent and summed in bfloat16 or wider, within the bound.
A program may use at most 384 MiB of HBM per device.

```python
import math
import jax
import jax.numpy as jnp
import numpy as np

FP = 16384
H1 = 2048
H2 = 1024
SYN_DEV = 1024
SYNTHONS = 8192
PRODUCTS = 16384
N_PROD = 8


def set_ends(entries, stream_key, least, high):
    extent = entries.shape
    index_at = [jax.random.randint(jax.random.fold_in(stream_key, axis), (), 0, extent[axis]) for axis in range(len(extent))]
    entries = entries.at[tuple(index_at)].set(least)
    longest = extent.index(max(extent))
    index_at[longest] = (index_at[longest] + 1) % extent[longest]
    return entries.at[tuple(index_at)].set(high)


def block_levels(key, dims, cuts, smallest, largest):
    def one(dim, blocks):
        steps = jax.random.uniform(jax.random.fold_in(jax.random.fold_in(key, 6), dim), (blocks,), jnp.float32, smallest / len(cuts), largest / len(cuts))
        return jnp.repeat(jnp.exp(steps), dims[dim] // blocks).reshape((-1,) + (1,) * (len(dims) - dim - 1))

    level = one(*cuts[0])
    for cut in cuts[1:]:
        level = level * one(*cut)
    return level


def rank_table(count, slope):
    portions = [(1 << 20) // math.isqrt(standing ** slope) + 1 for standing in range(1, count + 1)]
    scale = 1 + sum(portions) // (1 << 30)
    return np.cumsum(np.array([max(1, weight // scale) for weight in portions]))


def skewed_ids(stream_key, shape, count, skew):
    grid = rank_table(count, skew)
    pick = jax.random.randint(jax.random.fold_in(stream_key, 1), shape, 0, int(grid[count - 1]))
    standing = jnp.searchsorted(jnp.asarray(grid, jnp.int32), pick, side="right")
    return jax.random.permutation(jax.random.fold_in(stream_key, 2), count)[standing].astype(jnp.int32)


def scatter_about(key, shape, deviation, reach, cuts=(), held_as=jnp.bfloat16):
    values = jax.random.normal(key, shape, jnp.float32) * deviation
    if len(cuts) > 0:
        values = block_levels(key, shape, cuts, -0.22, 0.18) * values
    return jnp.clip(values, min=-reach, max=reach).astype(held_as)


def setup_inputs(seed: int = 0) -> dict:
    key_of = jax.random.split(jax.random.key(seed), 10)
    fingerprints = jnp.clip(3.0 * jax.random.uniform(key_of[0], (SYNTHONS, FP), jnp.float32) ** block_levels(key_of[0], (SYNTHONS, FP), ((0, 8),), -0.2, 0.2), 0.0, 3.0).astype(jnp.bfloat16)
    w_first = scatter_about(key_of[1], (FP, H1), FP ** -0.5, 0.046875, ((1, 4),))
    b_first = scatter_about(key_of[2], (H1,), 1.0, 4.0, ((0, 4),), jnp.float32)
    w_second = scatter_about(key_of[3], (H1, H2), H1 ** -0.5, 0.125)
    b_second = scatter_about(key_of[4], (H2,), 1.0, 4.0, (), jnp.float32)
    w_third = scatter_about(key_of[5], (H2,), H2 ** -0.5, 0.1875, (), jnp.float32)
    synth_block = set_ends(skewed_ids(key_of[6], (PRODUCTS, 3), N_PROD, 2), jax.random.fold_in(key_of[6], 3), 0, N_PROD - 1).astype(jnp.int32)
    synth_row = set_ends(jax.random.randint(key_of[7], (PRODUCTS, 3), 0, SYN_DEV), jax.random.fold_in(key_of[7], 1), 0, SYN_DEV - 1).astype(jnp.int32)
    third_used = set_ends((jax.random.randint(key_of[8], (PRODUCTS,), 0, 3) < 2).astype(jnp.int32), jax.random.fold_in(key_of[8], 1), 0, 1)
    return {"fingerprints": fingerprints, "w_first": w_first, "b_first": b_first, "w_second": w_second, "b_second": b_second, "w_third": w_third, "synth_block": synth_block, "synth_row": synth_row, "third_used": third_used}


def gelu_tanh(value):
    return 0.5 * value * (1.0 + jnp.tanh(0.7978845608028654 * (value + 0.044715 * value * value * value)))


def reference(fingerprints, w_first, b_first, w_second, b_second, w_third, synth_block, synth_row, third_used):
    synth_hidden = jnp.dot(fingerprints, w_first, preferred_element_type=jnp.float32).astype(jnp.bfloat16)
    glob = (synth_block * SYN_DEV + synth_row).astype(jnp.int32)
    first = synth_hidden[glob[:, 0]].astype(jnp.float32)
    second_row = synth_hidden[glob[:, 1]].astype(jnp.float32)
    third = synth_hidden[glob[:, 2]].astype(jnp.float32)
    composed = first + second_row + third_used.astype(jnp.float32)[:, None] * third
    act = gelu_tanh(composed + b_first[None, :]).astype(jnp.bfloat16)
    second = jnp.dot(act, w_second, preferred_element_type=jnp.float32)
    out = gelu_tanh(second + b_second[None, :])
    return jnp.sum(out * w_third[None, :], axis=1)
```

```python
import jax
import jax.numpy as jnp
from jax import lax
from jax.sharding import PartitionSpec as P


def gelu_tanh(value):
    return (
        0.5
        * value
        * (1.0 + jnp.tanh(0.7978845608028654 * (value + 0.044715 * value * value * value)))
    )


def local(
    fingerprints, w_first, b_first, w_second, b_second, w_third, synth_block, synth_row, third_used
):
    syn_rows = fingerprints.shape[0]
    prod_rows = synth_block.shape[0]
    synth_hidden = jnp.dot(fingerprints, w_first, preferred_element_type=jnp.float32).astype(
        jnp.bfloat16
    )
    glob = synth_block * syn_rows + synth_row
    ones_col = jnp.ones((prod_rows, 1), jnp.int32)
    live = jnp.concatenate([ones_col, ones_col, third_used[:, None]], axis=1)
    piece = lax.all_gather(synth_hidden, "prod", axis=0, tiled=True)
    columns = lax.iota(jnp.int32, piece.shape[0])
    hits = jnp.where(glob[:, :, None] == columns[None, None, :], live[:, :, None], 0)
    select = jnp.sum(hits, axis=1).astype(jnp.bfloat16)
    composed = jnp.dot(select, piece, preferred_element_type=jnp.float32)
    act = gelu_tanh(composed + b_first[None, :]).astype(jnp.bfloat16)
    traded = lax.all_to_all(act, "hid", split_axis=0, concat_axis=1, tiled=True)
    second = jnp.dot(traded, w_second, preferred_element_type=jnp.float32)
    out = gelu_tanh(second + b_second[None, :])
    return jnp.sum(out * w_third[None, :], axis=1)


def solution(mesh):
    placed = (
        P("prod", None),
        P(None, "hid"),
        P("hid"),
        P(),
        P(),
        P(),
        P("prod", None),
        P("prod", None),
        P("prod"),
    )
    return jax.shard_map(
        local, mesh=mesh, in_specs=placed, out_specs=P(("prod", "hid")), check_vma=False
    )
```

```python
import functools

import jax
import jax.numpy as jnp
from jax import lax
from jax.experimental import pallas as pl
from jax.experimental.pallas import tpu as pltpu
from jax.sharding import PartitionSpec as P

CHUNKS = 4
SLICES = 4
BUFFERS = 4
TILE = 16


def gelu_tanh(value):
    return (
        0.5
        * value
        * (1.0 + jnp.tanh(0.7978845608028654 * (value + 0.044715 * value * value * value)))
    )


def offsets(size):
    out = [(0, 0)]
    for far in range(1, size):
        out += [(far, far), (far, -far)]
    return out


def spread_kernel(nz, ny, fp_ref, w_ref, out_ref, w_all, fp_buf, acc, own, w_sem, fp_sem, own_sem, send_sem, recv_sem):
    me = lax.axis_index("prod")
    z, y = me // ny, me % ny
    rows = own.shape[0]
    step = rows // CHUNKS
    depth = w_ref.shape[0] // SLICES
    total = CHUNKS * SLICES

    def w_copy(k):
        part = pl.ds(pl.multiple_of(k * depth, depth), depth)
        return pltpu.make_async_copy(w_ref.at[part, :], w_all.at[part, :], w_sem.at[k])

    def fp_copy(s):
        slot = s % BUFFERS
        return pltpu.make_async_copy(
            fp_ref.at[
                pl.ds(pl.multiple_of((s // SLICES) * step, step), step),
                pl.ds(pl.multiple_of((s % SLICES) * depth, depth), depth),
            ],
            fp_buf.at[slot],
            fp_sem.at[slot],
        )

    for k in range(SLICES):
        w_copy(k).start()
        fp_copy(k).start()

    ways = (
        (z + 1 < nz, me + ny),
        (z >= 1, me - ny),
        (y + 1 < ny, me + 1),
        (y >= 1, me - 1),
    )
    barrier = pltpu.get_barrier_semaphore()
    count = jnp.int32(0)
    for there, target in ways:
        count = count + there.astype(jnp.int32)

        @pl.when(there)
        def _():
            pl.semaphore_signal(
                barrier, inc=1, device_id={"prod": target}, device_id_type=pl.DeviceIdType.MESH
            )

    pl.semaphore_wait(barrier, count)

    def place(src, c):
        return pl.ds(pl.multiple_of(src * rows + c * step, step), step)

    def send(c, zs, ys, mine, act):
        src = zs * ny + ys
        late = c == CHUNKS - 1
        in_col, in_row = y == ys, z == zs
        go_z = jnp.logical_or(in_col, late)
        go_y = jnp.logical_or(in_row, jnp.logical_not(late))
        want = (
            jnp.logical_and(go_z, z >= zs),
            jnp.logical_and(go_z, z <= zs),
            jnp.logical_and(go_y, y >= ys),
            jnp.logical_and(go_y, y <= ys),
        )
        for way, ((there, target), wish) in enumerate(zip(ways, want)):

            @pl.when(jnp.logical_and(there, wish))
            def _():
                source = (
                    own.at[pl.ds(pl.multiple_of(c * step, step), step), :]
                    if mine
                    else out_ref.at[place(src, c), :]
                )
                copy = pltpu.make_async_remote_copy(
                    src_ref=source,
                    dst_ref=out_ref.at[place(src, c), :],
                    send_sem=send_sem.at[way, src, c],
                    recv_sem=recv_sem.at[src, c],
                    device_id={"prod": target},
                    device_id_type=pl.DeviceIdType.MESH,
                )
                if act:
                    copy.start()
                else:
                    copy.wait_send()

    def keep(t):
        part = pl.ds(pl.multiple_of(t * step, step), step)
        return pltpu.make_async_copy(own.at[part, :], out_ref.at[place(me, t), :], own_sem.at[t])

    def compute(t, carry):
        def one(k, carry):
            s = t * SLICES + k

            @pl.when(t == 0)
            def _():
                w_copy(k).wait()

            fp_copy(s).wait()
            part = pl.ds(pl.multiple_of(k * depth, depth), depth)
            term = jnp.dot(fp_buf[s % BUFFERS], w_all[part, :], preferred_element_type=jnp.float32)

            @pl.when(k == 0)
            def _():
                acc[...] = term

            @pl.when(k > 0)
            def _():
                acc[...] += term

            @pl.when(s + BUFFERS < total)
            def _():
                fp_copy(s + BUFFERS).start()

            return carry

        lax.fori_loop(0, SLICES, one, 0)
        own[pl.ds(pl.multiple_of(t * step, step), step), :] = acc[...].astype(jnp.bfloat16)
        send(t, z, y, True, True)
        keep(t).start()
        return carry

    apart = [
        (dz, dy, far_z + far_y)
        for (far_z, dz) in offsets(nz)
        for (far_y, dy) in offsets(ny)
        if far_z + far_y > 0
    ]
    apart.sort(key=lambda item: item[2])
    furthest = apart[-1][2]

    def visit(c, act, dz, dy):
        zs, ys = z + dz, y + dy
        inside = (zs >= 0) & (zs < nz) & (ys >= 0) & (ys < ny) & (c >= 0) & (c < CHUNKS)

        @pl.when(inside)
        def _():
            if act:
                src = zs * ny + ys
                pltpu.make_async_copy(
                    out_ref.at[place(src, c), :], out_ref.at[place(src, c), :], recv_sem.at[src, c]
                ).wait()
            send(c, zs, ys, False, act)

    def turn(r, carry):
        for dz, dy, far in apart:
            visit(r - (far - 1), True, dz, dy)
        return carry

    lax.fori_loop(0, 2, compute, 0)
    turn(0, 0)
    lax.fori_loop(2, CHUNKS, compute, 0)
    lax.fori_loop(1, CHUNKS + furthest - 1, turn, 0)

    def finish(c, carry):
        send(c, z, y, True, False)
        keep(c).wait()
        for dz, dy, _ in apart:
            visit(c, False, dz, dy)
        return carry

    lax.fori_loop(0, CHUNKS, finish, 0)


def spread(fingerprints, w_first, prod):
    rows, depth = fingerprints.shape
    units = w_first.shape[1]
    nz = 4 if prod % 4 == 0 else 1
    ny = prod // nz
    return pl.pallas_call(
        functools.partial(spread_kernel, nz, ny),
        out_shape=jax.ShapeDtypeStruct((rows * prod, units), jnp.bfloat16),
        in_specs=[pl.BlockSpec(memory_space=pl.ANY)] * 2,
        out_specs=pl.BlockSpec(memory_space=pl.ANY),
        scratch_shapes=[
            pltpu.VMEM((depth, units), jnp.bfloat16),
            pltpu.VMEM((BUFFERS, rows // CHUNKS, depth // SLICES), jnp.bfloat16),
            pltpu.VMEM((rows // CHUNKS, units), jnp.float32),
            pltpu.VMEM((rows, units), jnp.bfloat16),
            pltpu.SemaphoreType.DMA((SLICES,)),
            pltpu.SemaphoreType.DMA((BUFFERS,)),
            pltpu.SemaphoreType.DMA((CHUNKS,)),
            pltpu.SemaphoreType.DMA((4, prod, CHUNKS)),
            pltpu.SemaphoreType.DMA((prod, CHUNKS)),
        ],
        compiler_params=pltpu.CompilerParams(
            collective_id=0, has_side_effects=True, vmem_limit_bytes=48 << 20
        ),
        cost_estimate=pl.CostEstimate(
            flops=2 * rows * depth * units,
            bytes_accessed=2 * (rows * depth + depth * units + rows * prod * units),
            transcendentals=0,
        ),
    )(fingerprints, w_first)


def pick_kernel(idx_ref, piece_ref, bias_ref, act_ref, table, land, group, sem):
    count = piece_ref.shape[0]
    step = land.shape[1]
    prods = act_ref.shape[0]
    steps = count // step

    def fetch(s):
        return pltpu.make_async_copy(
            piece_ref.at[pl.ds(pl.multiple_of(s * step, step), step), :],
            land.at[s % 4],
            sem.at[s % 4],
        )

    for s in range(4):
        fetch(s).start()
    table[count:, :] = jnp.zeros((table.shape[0] - count, table.shape[1]), jnp.float32)

    def widen(s, carry):
        fetch(s).wait()
        table[pl.ds(pl.multiple_of(s * step, step), step), :] = land[s % 4].astype(jnp.float32)

        @pl.when(s + 4 < steps)
        def _():
            fetch(s + 4).start()

        return carry

    lax.fori_loop(0, steps, widen, 0)
    bias = bias_ref[...]

    def some(i, carry):
        for j in range(TILE):
            p = i * TILE + j
            row = table[pl.ds(idx_ref[p], 1), :] + table[pl.ds(idx_ref[prods + p], 1), :]
            group[pl.ds(j, 1), :] = row + table[pl.ds(idx_ref[2 * prods + p], 1), :]
        act_ref[pl.ds(pl.multiple_of(i * TILE, TILE), TILE), :] = gelu_tanh(
            group[...] + bias
        ).astype(jnp.bfloat16)
        return carry

    lax.fori_loop(0, prods // TILE, some, 0)


def pick(idx, piece, bias):
    prods = idx.shape[0] // 3
    count, units = piece.shape
    step = min(512, count // 4)
    return pl.pallas_call(
        pick_kernel,
        out_shape=jax.ShapeDtypeStruct((prods, units), jnp.bfloat16),
        in_specs=[
            pl.BlockSpec(memory_space=pltpu.SMEM),
            pl.BlockSpec(memory_space=pl.ANY),
            pl.BlockSpec(memory_space=pltpu.VMEM),
        ],
        out_specs=pl.BlockSpec(memory_space=pltpu.VMEM),
        scratch_shapes=[
            pltpu.VMEM((count + 8, units), jnp.float32),
            pltpu.VMEM((4, step, units), jnp.bfloat16),
            pltpu.VMEM((TILE, units), jnp.float32),
            pltpu.SemaphoreType.DMA((4,)),
        ],
        compiler_params=pltpu.CompilerParams(vmem_limit_bytes=48 << 20),
    )(idx, piece, bias)


def local(
    prod, fingerprints, w_first, b_first, w_second, b_second, w_third, synth_block, synth_row, third_used
):
    syn_rows = fingerprints.shape[0]
    piece = spread(fingerprints, w_first, prod)
    glob = synth_block * syn_rows + synth_row
    third = jnp.where(third_used > 0, glob[:, 2], syn_rows * prod)
    idx = jnp.concatenate([glob[:, 0], glob[:, 1], third])
    act = pick(idx, piece, b_first[None, :])
    traded = lax.all_to_all(act, "hid", split_axis=0, concat_axis=1, tiled=True)
    second = jnp.dot(traded, w_second, preferred_element_type=jnp.float32)
    out = gelu_tanh(second + b_second[None, :])
    return jnp.sum(out * w_third[None, :], axis=1)


def solution(mesh):
    placed = (
        P("prod", None),
        P(None, "hid"),
        P("hid"),
        P(),
        P(),
        P(),
        P("prod", None),
        P("prod", None),
        P("prod"),
    )
    return jax.shard_map(
        functools.partial(local, mesh.shape["prod"]),
        mesh=mesh,
        in_specs=placed,
        out_specs=P(("prod", "hid")),
        check_vma=False,
    )
```

```python
import functools

import jax
import jax.numpy as jnp
from jax import lax
from jax.experimental import pallas as pl
from jax.experimental.pallas import tpu as pltpu
from jax.sharding import PartitionSpec as P

CHUNKS = 4
SLICES = 4
BUFFERS = 4
TILE = 16
PARTS = 4


def gelu_tanh(value):
    return (
        0.5
        * value
        * (1.0 + jnp.tanh(0.7978845608028654 * (value + 0.044715 * value * value * value)))
    )


def offsets(size):
    out = [(0, 0)]
    for far in range(1, size):
        out += [(far, far), (far, -far)]
    return out


def spread_kernel(nz, ny, fp_ref, w_ref, out_ref, w_all, fp_buf, acc, own, w_sem, fp_sem, own_sem, send_sem, recv_sem):
    me = lax.axis_index("prod")
    z, y = me // ny, me % ny
    rows = own.shape[0]
    step = rows // CHUNKS
    depth = w_ref.shape[0] // SLICES
    total = CHUNKS * SLICES

    def w_copy(k):
        part = pl.ds(pl.multiple_of(k * depth, depth), depth)
        return pltpu.make_async_copy(w_ref.at[part, :], w_all.at[part, :], w_sem.at[k])

    def fp_copy(s):
        slot = s % BUFFERS
        return pltpu.make_async_copy(
            fp_ref.at[
                pl.ds(pl.multiple_of((s // SLICES) * step, step), step),
                pl.ds(pl.multiple_of((s % SLICES) * depth, depth), depth),
            ],
            fp_buf.at[slot],
            fp_sem.at[slot],
        )

    for k in range(SLICES):
        w_copy(k).start()
        fp_copy(k).start()

    ways = (
        (z + 1 < nz, me + ny),
        (z >= 1, me - ny),
        (y + 1 < ny, me + 1),
        (y >= 1, me - 1),
    )
    barrier = pltpu.get_barrier_semaphore()
    count = jnp.int32(0)
    for there, target in ways:
        count = count + there.astype(jnp.int32)

        @pl.when(there)
        def _():
            pl.semaphore_signal(
                barrier, inc=1, device_id={"prod": target}, device_id_type=pl.DeviceIdType.MESH
            )

    pl.semaphore_wait(barrier, count)

    def place(src, c):
        return pl.ds(pl.multiple_of(src * rows + c * step, step), step)

    def send(c, zs, ys, mine, act):
        src = zs * ny + ys
        late = c == CHUNKS - 1
        in_col, in_row = y == ys, z == zs
        go_z = jnp.logical_or(in_col, late)
        go_y = jnp.logical_or(in_row, jnp.logical_not(late))
        want = (
            jnp.logical_and(go_z, z >= zs),
            jnp.logical_and(go_z, z <= zs),
            jnp.logical_and(go_y, y >= ys),
            jnp.logical_and(go_y, y <= ys),
        )
        for way, ((there, target), wish) in enumerate(zip(ways, want)):

            @pl.when(jnp.logical_and(there, wish))
            def _():
                source = (
                    own.at[pl.ds(pl.multiple_of(c * step, step), step), :]
                    if mine
                    else out_ref.at[place(src, c), :]
                )
                copy = pltpu.make_async_remote_copy(
                    src_ref=source,
                    dst_ref=out_ref.at[place(src, c), :],
                    send_sem=send_sem.at[way, src, c],
                    recv_sem=recv_sem.at[src, c],
                    device_id={"prod": target},
                    device_id_type=pl.DeviceIdType.MESH,
                )
                if act:
                    copy.start()
                else:
                    copy.wait_send()

    def keep(t):
        part = pl.ds(pl.multiple_of(t * step, step), step)
        return pltpu.make_async_copy(own.at[part, :], out_ref.at[place(me, t), :], own_sem.at[t])

    def compute(t, carry):
        def one(k, carry):
            s = t * SLICES + k

            @pl.when(t == 0)
            def _():
                w_copy(k).wait()

            fp_copy(s).wait()
            part = pl.ds(pl.multiple_of(k * depth, depth), depth)
            term = jnp.dot(fp_buf[s % BUFFERS], w_all[part, :], preferred_element_type=jnp.float32)

            @pl.when(k == 0)
            def _():
                acc[...] = term

            @pl.when(k > 0)
            def _():
                acc[...] += term

            @pl.when(s + BUFFERS < total)
            def _():
                fp_copy(s + BUFFERS).start()

            return carry

        lax.fori_loop(0, SLICES, one, 0)
        own[pl.ds(pl.multiple_of(t * step, step), step), :] = acc[...].astype(jnp.bfloat16)
        send(t, z, y, True, True)
        keep(t).start()
        return carry

    apart = [
        (dz, dy, far_z + far_y)
        for (far_z, dz) in offsets(nz)
        for (far_y, dy) in offsets(ny)
        if far_z + far_y > 0
    ]
    apart.sort(key=lambda item: item[2])
    furthest = apart[-1][2]

    def visit(c, act, dz, dy):
        zs, ys = z + dz, y + dy
        inside = (zs >= 0) & (zs < nz) & (ys >= 0) & (ys < ny) & (c >= 0) & (c < CHUNKS)

        @pl.when(inside)
        def _():
            if act:
                src = zs * ny + ys
                pltpu.make_async_copy(
                    out_ref.at[place(src, c), :], out_ref.at[place(src, c), :], recv_sem.at[src, c]
                ).wait()
            send(c, zs, ys, False, act)

    def turn(r, carry):
        for dz, dy, far in apart:
            visit(r - (far - 1), True, dz, dy)
        return carry

    lax.fori_loop(0, 2, compute, 0)
    turn(0, 0)
    lax.fori_loop(2, CHUNKS, compute, 0)
    lax.fori_loop(1, CHUNKS + furthest - 1, turn, 0)

    def finish(c, carry):
        send(c, z, y, True, False)
        keep(c).wait()
        for dz, dy, _ in apart:
            visit(c, False, dz, dy)
        return carry

    lax.fori_loop(0, CHUNKS, finish, 0)


def spread(fingerprints, w_first, prod):
    rows, depth = fingerprints.shape
    units = w_first.shape[1]
    nz = 4 if prod % 4 == 0 else 1
    ny = prod // nz
    return pl.pallas_call(
        functools.partial(spread_kernel, nz, ny),
        out_shape=jax.ShapeDtypeStruct((rows * prod, units), jnp.bfloat16),
        in_specs=[pl.BlockSpec(memory_space=pl.ANY)] * 2,
        out_specs=pl.BlockSpec(memory_space=pl.ANY),
        scratch_shapes=[
            pltpu.VMEM((depth, units), jnp.bfloat16),
            pltpu.VMEM((BUFFERS, rows // CHUNKS, depth // SLICES), jnp.bfloat16),
            pltpu.VMEM((rows // CHUNKS, units), jnp.float32),
            pltpu.VMEM((rows, units), jnp.bfloat16),
            pltpu.SemaphoreType.DMA((SLICES,)),
            pltpu.SemaphoreType.DMA((BUFFERS,)),
            pltpu.SemaphoreType.DMA((CHUNKS,)),
            pltpu.SemaphoreType.DMA((4, prod, CHUNKS)),
            pltpu.SemaphoreType.DMA((prod, CHUNKS)),
        ],
        compiler_params=pltpu.CompilerParams(
            collective_id=0, has_side_effects=True, vmem_limit_bytes=48 << 20
        ),
        cost_estimate=pl.CostEstimate(
            flops=2 * rows * depth * units,
            bytes_accessed=2 * (rows * depth + depth * units + rows * prod * units),
            transcendentals=0,
        ),
    )(fingerprints, w_first)


def pick_kernel(
    hid, idx_ref, piece_ref, bias_ref, w_ref, b_ref, out_w_ref, score_ref, table, land, group, act, got, total, sem, send_sem, recv_sem
):
    me = lax.axis_index("hid")
    chips = hid // 2
    count = piece_ref.shape[0]
    step = land.shape[1]
    prods, units = act.shape
    share = prods // hid
    part = share // PARTS
    steps = count // step

    def fetch(s):
        return pltpu.make_async_copy(
            piece_ref.at[pl.ds(pl.multiple_of(s * step, step), step), :],
            land.at[s % 4],
            sem.at[s % 4],
        )

    for s in range(4):
        fetch(s).start()
    barrier = pltpu.get_barrier_semaphore()
    for j in range(1, hid):
        pl.semaphore_signal(
            barrier, inc=1, device_id={"hid": (me + j) % hid}, device_id_type=pl.DeviceIdType.MESH
        )
    table[count:, :] = jnp.zeros((table.shape[0] - count, units), jnp.float32)

    def widen(s, carry):
        fetch(s).wait()
        table[pl.ds(pl.multiple_of(s * step, step), step), :] = land[s % 4].astype(jnp.float32)

        @pl.when(s + 4 < steps)
        def _():
            fetch(s + 4).start()

        return carry

    lax.fori_loop(0, steps, widen, 0)
    pl.semaphore_wait(barrier, hid - 1)
    bias = bias_ref[...]

    def target(d):
        chip = (me // 2 + d // 2 + 1) % chips
        return chip * 2 + (me % 2 + 1 + d) % 2

    def send(dest, c):
        return pltpu.make_async_remote_copy(
            src_ref=act.at[pl.ds(pl.multiple_of(dest * share + c * part, part), part), :],
            dst_ref=got.at[me, pl.ds(pl.multiple_of(c * part, part), part), :],
            send_sem=send_sem.at[dest, c],
            recv_sem=recv_sem.at[me, c],
            device_id={"hid": dest},
            device_id_type=pl.DeviceIdType.MESH,
        )

    def block(n, carry):
        dest, c = target(n // PARTS), n % PARTS
        first = dest * share + c * part

        def some(i, carry):
            base = first + i * TILE
            for j in range(TILE):
                p = base + j
                row = table[pl.ds(idx_ref[p], 1), :] + table[pl.ds(idx_ref[prods + p], 1), :]
                group[pl.ds(j, 1), :] = row + table[pl.ds(idx_ref[2 * prods + p], 1), :]
            act[pl.ds(pl.multiple_of(base, TILE), TILE), :] = gelu_tanh(group[...] + bias).astype(
                jnp.bfloat16
            )
            return carry

        lax.fori_loop(0, part // TILE, some, 0)

        @pl.when(dest != me)
        def _():
            send(dest, c).start()

        return carry

    lax.fori_loop(0, hid * PARTS, block, 0)

    def weights(source):
        return w_ref[pl.ds(pl.multiple_of(source * units, units), units), :]

    mine = act[pl.ds(pl.multiple_of(me * share, share), share), :]
    total[...] = jnp.dot(mine, weights(me), preferred_element_type=jnp.float32)

    def add(d, carry):
        source = target((d + hid - 2) % hid)
        for c in range(PARTS):
            pltpu.make_async_copy(
                got.at[source, pl.ds(c * part, part), :],
                got.at[source, pl.ds(c * part, part), :],
                recv_sem.at[source, c],
            ).wait()
        total[...] += jnp.dot(got[source], weights(source), preferred_element_type=jnp.float32)
        return carry

    add(0, 0)
    lax.fori_loop(2, hid, add, 0)
    last = gelu_tanh(total[...] + b_ref[...]) * out_w_ref[...]
    score_ref[...] = jnp.sum(last, axis=1, keepdims=True)

    def done(n, carry):
        send(target(n // PARTS), n % PARTS).wait_send()
        return carry

    lax.fori_loop(0, (hid - 1) * PARTS, done, 0)


def pick(hid, idx, piece, bias, w_second, b_second, w_third):
    prods = idx.shape[0] // 3
    count, units = piece.shape
    wide = w_second.shape[1]
    share = prods // hid
    step = min(512, count // 4)
    return pl.pallas_call(
        functools.partial(pick_kernel, hid),
        out_shape=jax.ShapeDtypeStruct((share, 1), jnp.float32),
        in_specs=[
            pl.BlockSpec(memory_space=pltpu.SMEM),
            pl.BlockSpec(memory_space=pl.ANY),
        ]
        + [pl.BlockSpec(memory_space=pltpu.VMEM)] * 4,
        out_specs=pl.BlockSpec(memory_space=pltpu.VMEM),
        scratch_shapes=[
            pltpu.VMEM((count + 8, units), jnp.float32),
            pltpu.VMEM((4, step, units), jnp.bfloat16),
            pltpu.VMEM((TILE, units), jnp.float32),
            pltpu.VMEM((prods, units), jnp.bfloat16),
            pltpu.VMEM((hid, share, units), jnp.bfloat16),
            pltpu.VMEM((share, wide), jnp.float32),
            pltpu.SemaphoreType.DMA((4,)),
            pltpu.SemaphoreType.DMA((hid, PARTS)),
            pltpu.SemaphoreType.DMA((hid, PARTS)),
        ],
        compiler_params=pltpu.CompilerParams(
            collective_id=1, has_side_effects=True, vmem_limit_bytes=48 << 20
        ),
    )(idx, piece, bias, w_second, b_second, w_third)


def local(
    prod, hid, fingerprints, w_first, b_first, w_second, b_second, w_third, synth_block, synth_row, third_used
):
    syn_rows = fingerprints.shape[0]
    piece = spread(fingerprints, w_first, prod)
    glob = synth_block * syn_rows + synth_row
    third = jnp.where(third_used > 0, glob[:, 2], syn_rows * prod)
    idx = jnp.concatenate([glob[:, 0], glob[:, 1], third])
    score = pick(
        hid, idx, piece, b_first[None, :], w_second, b_second[None, :], w_third[None, :]
    )
    return score.reshape(-1)


def solution(mesh):
    placed = (
        P("prod", None),
        P(None, "hid"),
        P("hid"),
        P(),
        P(),
        P(),
        P("prod", None),
        P("prod", None),
        P("prod"),
    )
    return jax.shard_map(
        functools.partial(local, mesh.shape["prod"], mesh.shape["hid"]),
        mesh=mesh,
        in_specs=placed,
        out_specs=P(("prod", "hid")),
        check_vma=False,
    )
```

```python
import functools

import jax
import jax.numpy as jnp
from jax import lax
from jax.experimental import pallas as pl
from jax.experimental.pallas import tpu as pltpu
from jax.sharding import PartitionSpec as P

CHUNKS = 8
SLICES = 4
BUFFERS = 8
TILE = 16
PARTS = 4


def gelu_tanh(value):
    return (
        0.5
        * value
        * (1.0 + jnp.tanh(0.7978845608028654 * (value + 0.044715 * value * value * value)))
    )


def offsets(size):
    out = [(0, 0)]
    for far in range(1, size):
        out += [(far, far), (far, -far)]
    return out


def spread_kernel(nz, ny, fp_ref, w_ref, out_ref, w_all, fp_buf, acc, own, w_sem, fp_sem, own_sem, send_sem, recv_sem):
    me = lax.axis_index("prod")
    z, y = me // ny, me % ny
    rows = own.shape[0]
    step = rows // CHUNKS
    depth = w_ref.shape[0] // SLICES
    total = CHUNKS * SLICES

    def w_copy(k):
        part = pl.ds(pl.multiple_of(k * depth, depth), depth)
        return pltpu.make_async_copy(w_ref.at[part, :], w_all.at[part, :], w_sem.at[k])

    def fp_copy(s):
        slot = s % BUFFERS
        return pltpu.make_async_copy(
            fp_ref.at[
                pl.ds(pl.multiple_of((s // SLICES) * step, step), step),
                pl.ds(pl.multiple_of((s % SLICES) * depth, depth), depth),
            ],
            fp_buf.at[slot],
            fp_sem.at[slot],
        )

    for k in range(SLICES):
        w_copy(k).start()
        fp_copy(k).start()
    for k in range(SLICES, BUFFERS):
        fp_copy(k).start()

    ways = (
        (z + 1 < nz, me + ny),
        (z >= 1, me - ny),
        (y + 1 < ny, me + 1),
        (y >= 1, me - 1),
    )
    barrier = pltpu.get_barrier_semaphore()
    count = jnp.int32(0)
    for there, target in ways:
        count = count + there.astype(jnp.int32)

        @pl.when(there)
        def _():
            pl.semaphore_signal(
                barrier, inc=1, device_id={"prod": target}, device_id_type=pl.DeviceIdType.MESH
            )

    pl.semaphore_wait(barrier, count)

    def place(src, c):
        return pl.ds(pl.multiple_of(src * rows + c * step, step), step)

    def send(c, zs, ys, mine, act):
        src = zs * ny + ys
        late = c == CHUNKS - 1
        in_col, in_row = y == ys, z == zs
        go_z = jnp.logical_or(in_col, late)
        go_y = jnp.logical_or(in_row, jnp.logical_not(late))
        want = (
            jnp.logical_and(go_z, z >= zs),
            jnp.logical_and(go_z, z <= zs),
            jnp.logical_and(go_y, y >= ys),
            jnp.logical_and(go_y, y <= ys),
        )
        for way, ((there, target), wish) in enumerate(zip(ways, want)):

            @pl.when(jnp.logical_and(there, wish))
            def _():
                source = (
                    own.at[pl.ds(pl.multiple_of(c * step, step), step), :]
                    if mine
                    else out_ref.at[place(src, c), :]
                )
                copy = pltpu.make_async_remote_copy(
                    src_ref=source,
                    dst_ref=out_ref.at[place(src, c), :],
                    send_sem=send_sem.at[way, src, c],
                    recv_sem=recv_sem.at[src, c],
                    device_id={"prod": target},
                    device_id_type=pl.DeviceIdType.MESH,
                )
                if act:
                    copy.start()
                else:
                    copy.wait_send()

    def keep(t):
        part = pl.ds(pl.multiple_of(t * step, step), step)
        return pltpu.make_async_copy(own.at[part, :], out_ref.at[place(me, t), :], own_sem.at[t])

    def compute(t, carry):
        def one(k, carry):
            s = t * SLICES + k

            @pl.when(t == 0)
            def _():
                w_copy(k).wait()

            fp_copy(s).wait()
            part = pl.ds(pl.multiple_of(k * depth, depth), depth)
            term = jnp.dot(fp_buf[s % BUFFERS], w_all[part, :], preferred_element_type=jnp.float32)

            @pl.when(k == 0)
            def _():
                acc[...] = term

            @pl.when(k > 0)
            def _():
                acc[...] += term

            @pl.when(s + BUFFERS < total)
            def _():
                fp_copy(s + BUFFERS).start()

            return carry

        lax.fori_loop(0, SLICES, one, 0)
        own[pl.ds(pl.multiple_of(t * step, step), step), :] = acc[...].astype(jnp.bfloat16)
        send(t, z, y, True, True)
        keep(t).start()
        return carry

    apart = [
        (dz, dy, far_z + far_y)
        for (far_z, dz) in offsets(nz)
        for (far_y, dy) in offsets(ny)
        if far_z + far_y > 0
    ]
    apart.sort(key=lambda item: item[2])
    furthest = apart[-1][2]

    def visit(c, act, dz, dy):
        zs, ys = z + dz, y + dy
        inside = (zs >= 0) & (zs < nz) & (ys >= 0) & (ys < ny) & (c >= 0) & (c < CHUNKS)

        @pl.when(inside)
        def _():
            if act:
                src = zs * ny + ys
                pltpu.make_async_copy(
                    out_ref.at[place(src, c), :], out_ref.at[place(src, c), :], recv_sem.at[src, c]
                ).wait()
            send(c, zs, ys, False, act)

    def turn(r, carry):
        for dz, dy, far in apart:
            visit(r - (far - 1), True, dz, dy)
        return carry

    def both(r, carry):
        lax.fori_loop(2 * r, 2 * r + 2, compute, 0)
        return turn(r, carry)

    lax.fori_loop(0, CHUNKS // 2, both, 0)
    lax.fori_loop(CHUNKS // 2, CHUNKS + furthest - 1, turn, 0)

    def finish(c, carry):
        send(c, z, y, True, False)
        keep(c).wait()
        for dz, dy, _ in apart:
            visit(c, False, dz, dy)
        return carry

    lax.fori_loop(0, CHUNKS, finish, 0)


def spread(fingerprints, w_first, prod):
    rows, depth = fingerprints.shape
    units = w_first.shape[1]
    nz = 4 if prod % 4 == 0 else 1
    ny = prod // nz
    return pl.pallas_call(
        functools.partial(spread_kernel, nz, ny),
        out_shape=jax.ShapeDtypeStruct((rows * prod, units), jnp.bfloat16),
        in_specs=[pl.BlockSpec(memory_space=pl.ANY)] * 2,
        out_specs=pl.BlockSpec(memory_space=pl.ANY),
        scratch_shapes=[
            pltpu.VMEM((depth, units), jnp.bfloat16),
            pltpu.VMEM((BUFFERS, rows // CHUNKS, depth // SLICES), jnp.bfloat16),
            pltpu.VMEM((rows // CHUNKS, units), jnp.float32),
            pltpu.VMEM((rows, units), jnp.bfloat16),
            pltpu.SemaphoreType.DMA((SLICES,)),
            pltpu.SemaphoreType.DMA((BUFFERS,)),
            pltpu.SemaphoreType.DMA((CHUNKS,)),
            pltpu.SemaphoreType.DMA((4, prod, CHUNKS)),
            pltpu.SemaphoreType.DMA((prod, CHUNKS)),
        ],
        compiler_params=pltpu.CompilerParams(
            collective_id=0, has_side_effects=True, vmem_limit_bytes=48 << 20
        ),
        cost_estimate=pl.CostEstimate(
            flops=2 * rows * depth * units,
            bytes_accessed=2 * (rows * depth + depth * units + rows * prod * units),
            transcendentals=0,
        ),
    )(fingerprints, w_first)


def pick_kernel(
    hid, idx_ref, piece_ref, bias_ref, w_ref, b_ref, out_w_ref, score_ref, table, land, group, act, got, total, sem, send_sem, recv_sem
):
    me = lax.axis_index("hid")
    chips = hid // 2
    count = piece_ref.shape[0]
    step = land.shape[1]
    prods, units = act.shape
    share = prods // hid
    part = share // PARTS
    steps = count // step

    def fetch(s):
        return pltpu.make_async_copy(
            piece_ref.at[pl.ds(pl.multiple_of(s * step, step), step), :],
            land.at[s % 4],
            sem.at[s % 4],
        )

    for s in range(4):
        fetch(s).start()
    barrier = pltpu.get_barrier_semaphore()
    for j in range(1, hid):
        pl.semaphore_signal(
            barrier, inc=1, device_id={"hid": (me + j) % hid}, device_id_type=pl.DeviceIdType.MESH
        )
    table[count:, :] = jnp.zeros((table.shape[0] - count, units), jnp.float32)

    def widen(s, carry):
        fetch(s).wait()
        table[pl.ds(pl.multiple_of(s * step, step), step), :] = land[s % 4].astype(jnp.float32)

        @pl.when(s + 4 < steps)
        def _():
            fetch(s + 4).start()

        return carry

    lax.fori_loop(0, steps, widen, 0)
    pl.semaphore_wait(barrier, hid - 1)
    bias = bias_ref[...]

    def target(d):
        chip = (me // 2 + d // 2 + 1) % chips
        return chip * 2 + (me % 2 + 1 + d) % 2

    def send(dest, c):
        return pltpu.make_async_remote_copy(
            src_ref=act.at[pl.ds(pl.multiple_of(dest * share + c * part, part), part), :],
            dst_ref=got.at[me, pl.ds(pl.multiple_of(c * part, part), part), :],
            send_sem=send_sem.at[dest, c],
            recv_sem=recv_sem.at[me, c],
            device_id={"hid": dest},
            device_id_type=pl.DeviceIdType.MESH,
        )

    def block(n, carry):
        dest, c = target(n // PARTS), n % PARTS
        first = dest * share + c * part

        def some(i, carry):
            base = first + i * TILE
            for j in range(TILE):
                p = base + j
                row = table[pl.ds(idx_ref[p], 1), :] + table[pl.ds(idx_ref[prods + p], 1), :]
                group[pl.ds(j, 1), :] = row + table[pl.ds(idx_ref[2 * prods + p], 1), :]
            act[pl.ds(pl.multiple_of(base, TILE), TILE), :] = gelu_tanh(group[...] + bias).astype(
                jnp.bfloat16
            )
            return carry

        lax.fori_loop(0, part // TILE, some, 0)

        @pl.when(dest != me)
        def _():
            send(dest, c).start()

        return carry

    lax.fori_loop(0, hid * PARTS, block, 0)

    def weights(source):
        return w_ref[pl.ds(pl.multiple_of(source * units, units), units), :]

    mine = act[pl.ds(pl.multiple_of(me * share, share), share), :]
    total[...] = jnp.dot(mine, weights(me), preferred_element_type=jnp.float32)

    def add(d, carry):
        source = target((d + hid - 2) % hid)
        for c in range(PARTS):
            pltpu.make_async_copy(
                got.at[source, pl.ds(c * part, part), :],
                got.at[source, pl.ds(c * part, part), :],
                recv_sem.at[source, c],
            ).wait()
        total[...] += jnp.dot(got[source], weights(source), preferred_element_type=jnp.float32)
        return carry

    add(0, 0)
    lax.fori_loop(2, hid, add, 0)
    last = gelu_tanh(total[...] + b_ref[...]) * out_w_ref[...]
    score_ref[...] = jnp.sum(last, axis=1, keepdims=True)

    def done(n, carry):
        send(target(n // PARTS), n % PARTS).wait_send()
        return carry

    lax.fori_loop(0, (hid - 1) * PARTS, done, 0)


def pick(hid, idx, piece, bias, w_second, b_second, w_third):
    prods = idx.shape[0] // 3
    count, units = piece.shape
    wide = w_second.shape[1]
    share = prods // hid
    step = min(512, count // 4)
    return pl.pallas_call(
        functools.partial(pick_kernel, hid),
        out_shape=jax.ShapeDtypeStruct((share, 1), jnp.float32),
        in_specs=[
            pl.BlockSpec(memory_space=pltpu.SMEM),
            pl.BlockSpec(memory_space=pl.ANY),
        ]
        + [pl.BlockSpec(memory_space=pltpu.VMEM)] * 4,
        out_specs=pl.BlockSpec(memory_space=pltpu.VMEM),
        scratch_shapes=[
            pltpu.VMEM((count + 8, units), jnp.float32),
            pltpu.VMEM((4, step, units), jnp.bfloat16),
            pltpu.VMEM((TILE, units), jnp.float32),
            pltpu.VMEM((prods, units), jnp.bfloat16),
            pltpu.VMEM((hid, share, units), jnp.bfloat16),
            pltpu.VMEM((share, wide), jnp.float32),
            pltpu.SemaphoreType.DMA((4,)),
            pltpu.SemaphoreType.DMA((hid, PARTS)),
            pltpu.SemaphoreType.DMA((hid, PARTS)),
        ],
        compiler_params=pltpu.CompilerParams(
            collective_id=1, has_side_effects=True, vmem_limit_bytes=48 << 20
        ),
    )(idx, piece, bias, w_second, b_second, w_third)


def local(
    prod, hid, fingerprints, w_first, b_first, w_second, b_second, w_third, synth_block, synth_row, third_used
):
    syn_rows = fingerprints.shape[0]
    piece = spread(fingerprints, w_first, prod)
    glob = synth_block * syn_rows + synth_row
    third = jnp.where(third_used > 0, glob[:, 2], syn_rows * prod)
    idx = jnp.concatenate([glob[:, 0], glob[:, 1], third])
    score = pick(
        hid, idx, piece, b_first[None, :], w_second, b_second[None, :], w_third[None, :]
    )
    return score.reshape(-1)


def solution(mesh):
    placed = (
        P("prod", None),
        P(None, "hid"),
        P("hid"),
        P(),
        P(),
        P(),
        P("prod", None),
        P("prod", None),
        P("prod"),
    )
    return jax.shard_map(
        functools.partial(local, mesh.shape["prod"], mesh.shape["hid"]),
        mesh=mesh,
        in_specs=placed,
        out_specs=P(("prod", "hid")),
        check_vma=False,
    )
```

```python
import functools

import jax
import jax.numpy as jnp
from jax import lax
from jax.experimental import pallas as pl
from jax.experimental.pallas import tpu as pltpu
from jax.sharding import PartitionSpec as P

CHUNKS = 4
SLICES = 4
BUFFERS = 4
TILE = 16
PARTS = 4


def gelu_tanh(value):
    return (
        0.5
        * value
        * (1.0 + jnp.tanh(0.7978845608028654 * (value + 0.044715 * value * value * value)))
    )


def offsets(size):
    out = [(0, 0)]
    for far in range(1, size):
        out += [(far, far), (far, -far)]
    return out


def spread_kernel(nz, ny, fp_ref, w_ref, out_ref, w_all, fp_buf, acc, own, w_sem, fp_sem, own_sem, send_sem, recv_sem):
    me = lax.axis_index("prod")
    z, y = me // ny, me % ny
    rows = own.shape[0]
    step = rows // CHUNKS
    depth = w_ref.shape[0] // SLICES
    total = CHUNKS * SLICES

    def w_copy(k):
        part = pl.ds(pl.multiple_of(k * depth, depth), depth)
        return pltpu.make_async_copy(w_ref.at[part, :], w_all.at[part, :], w_sem.at[k])

    def fp_copy(s):
        slot = s % BUFFERS
        return pltpu.make_async_copy(
            fp_ref.at[
                pl.ds(pl.multiple_of((s // SLICES) * step, step), step),
                pl.ds(pl.multiple_of((s % SLICES) * depth, depth), depth),
            ],
            fp_buf.at[slot],
            fp_sem.at[slot],
        )

    for k in range(SLICES):
        w_copy(k).start()
        fp_copy(k).start()

    ways = (
        (z + 1 < nz, me + ny),
        (z >= 1, me - ny),
        (y + 1 < ny, me + 1),
        (y >= 1, me - 1),
    )
    barrier = pltpu.get_barrier_semaphore()
    count = jnp.int32(0)
    for there, target in ways:
        count = count + there.astype(jnp.int32)

        @pl.when(there)
        def _():
            pl.semaphore_signal(
                barrier, inc=1, device_id={"prod": target}, device_id_type=pl.DeviceIdType.MESH
            )

    pl.semaphore_wait(barrier, count)

    def place(src, c):
        return pl.ds(pl.multiple_of(src * rows + c * step, step), step)

    second = step * 3 // 256 * 16
    spans = ((0, step - second), (step - second, second))

    def piece_of(start, way):
        skip, size = spans[way]
        return pl.ds(pl.multiple_of(start + skip, 16), size)

    def arrived(src, c, order):
        there = out_ref.at[piece_of(src * rows + c * step, order), :]
        pltpu.make_async_copy(there, there, recv_sem.at[src, c * 2 + order]).wait()

    def send(c, zs, ys, mine, act):
        send_part(c, zs, ys, mine, act, 0)
        send_part(c, zs, ys, mine, act, 1)

    def send_part(c, zs, ys, mine, act, order):
        src = zs * ny + ys
        in_col, in_row = y == ys, z == zs
        go_z = in_col if order == 0 else (z >= 0)
        go_y = in_row if order == 1 else (y >= 0)
        want = (
            jnp.logical_and(go_z, z >= zs),
            jnp.logical_and(go_z, z <= zs),
            jnp.logical_and(go_y, y >= ys),
            jnp.logical_and(go_y, y <= ys),
        )
        for way, ((there, target), wish) in enumerate(zip(ways, want)):

            @pl.when(jnp.logical_and(there, wish))
            def _():
                source = (
                    own.at[piece_of(c * step, order), :]
                    if mine
                    else out_ref.at[piece_of(src * rows + c * step, order), :]
                )
                copy = pltpu.make_async_remote_copy(
                    src_ref=source,
                    dst_ref=out_ref.at[piece_of(src * rows + c * step, order), :],
                    send_sem=send_sem.at[way, src, c * 2 + order],
                    recv_sem=recv_sem.at[src, c * 2 + order],
                    device_id={"prod": target},
                    device_id_type=pl.DeviceIdType.MESH,
                )
                if act:
                    copy.start()
                else:
                    copy.wait_send()

    def keep(t):
        part = pl.ds(pl.multiple_of(t * step, step), step)
        return pltpu.make_async_copy(own.at[part, :], out_ref.at[place(me, t), :], own_sem.at[t])

    def compute(t, carry):
        def one(k, carry):
            s = t * SLICES + k

            @pl.when(t == 0)
            def _():
                w_copy(k).wait()

            fp_copy(s).wait()
            part = pl.ds(pl.multiple_of(k * depth, depth), depth)
            term = jnp.dot(fp_buf[s % BUFFERS], w_all[part, :], preferred_element_type=jnp.float32)

            @pl.when(k == 0)
            def _():
                acc[...] = term

            @pl.when(k > 0)
            def _():
                acc[...] += term

            @pl.when(s + BUFFERS < total)
            def _():
                fp_copy(s + BUFFERS).start()

            return carry

        lax.fori_loop(0, SLICES, one, 0)
        own[pl.ds(pl.multiple_of(t * step, step), step), :] = acc[...].astype(jnp.bfloat16)
        send(t, z, y, True, True)
        keep(t).start()
        return carry

    apart = [
        (dz, dy, far_z + far_y)
        for (far_z, dz) in offsets(nz)
        for (far_y, dy) in offsets(ny)
        if far_z + far_y > 0
    ]
    apart.sort(key=lambda item: item[2])
    furthest = apart[-1][2]

    def visit(c, act, dz, dy):
        zs, ys = z + dz, y + dy
        inside = (zs >= 0) & (zs < nz) & (ys >= 0) & (ys < ny) & (c >= 0) & (c < CHUNKS)

        @pl.when(inside)
        def _():
            for order in range(2):
                if act:
                    arrived(zs * ny + ys, c, order)
                send_part(c, zs, ys, False, act, order)

    def turn(r, carry):
        for dz, dy, far in apart:
            visit(r - (far - 1), True, dz, dy)
        return carry

    lax.fori_loop(0, 2, compute, 0)
    turn(0, 0)
    lax.fori_loop(2, CHUNKS, compute, 0)
    lax.fori_loop(1, CHUNKS + furthest - 1, turn, 0)

    def finish(c, carry):
        send(c, z, y, True, False)
        keep(c).wait()
        for dz, dy, _ in apart:
            visit(c, False, dz, dy)
        return carry

    lax.fori_loop(0, CHUNKS, finish, 0)


def spread(fingerprints, w_first, prod):
    rows, depth = fingerprints.shape
    units = w_first.shape[1]
    nz = 4 if prod % 4 == 0 else 1
    ny = prod // nz
    return pl.pallas_call(
        functools.partial(spread_kernel, nz, ny),
        out_shape=jax.ShapeDtypeStruct((rows * prod, units), jnp.bfloat16),
        in_specs=[pl.BlockSpec(memory_space=pl.ANY)] * 2,
        out_specs=pl.BlockSpec(memory_space=pl.ANY),
        scratch_shapes=[
            pltpu.VMEM((depth, units), jnp.bfloat16),
            pltpu.VMEM((BUFFERS, rows // CHUNKS, depth // SLICES), jnp.bfloat16),
            pltpu.VMEM((rows // CHUNKS, units), jnp.float32),
            pltpu.VMEM((rows, units), jnp.bfloat16),
            pltpu.SemaphoreType.DMA((SLICES,)),
            pltpu.SemaphoreType.DMA((BUFFERS,)),
            pltpu.SemaphoreType.DMA((CHUNKS,)),
            pltpu.SemaphoreType.DMA((4, prod, CHUNKS * 2)),
            pltpu.SemaphoreType.DMA((prod, CHUNKS * 2)),
        ],
        compiler_params=pltpu.CompilerParams(
            collective_id=0, has_side_effects=True, vmem_limit_bytes=48 << 20
        ),
        cost_estimate=pl.CostEstimate(
            flops=2 * rows * depth * units,
            bytes_accessed=2 * (rows * depth + depth * units + rows * prod * units),
            transcendentals=0,
        ),
    )(fingerprints, w_first)


def pick_kernel(
    hid, idx_ref, piece_ref, bias_ref, w_ref, b_ref, out_w_ref, score_ref, table, land, group, act, got, total, sem, send_sem, recv_sem
):
    me = lax.axis_index("hid")
    chips = hid // 2
    count = piece_ref.shape[0]
    step = land.shape[1]
    prods, units = act.shape
    share = prods // hid
    part = share // PARTS
    steps = count // step

    def fetch(s):
        return pltpu.make_async_copy(
            piece_ref.at[pl.ds(pl.multiple_of(s * step, step), step), :],
            land.at[s % 4],
            sem.at[s % 4],
        )

    for s in range(4):
        fetch(s).start()
    barrier = pltpu.get_barrier_semaphore()
    for j in range(1, hid):
        pl.semaphore_signal(
            barrier, inc=1, device_id={"hid": (me + j) % hid}, device_id_type=pl.DeviceIdType.MESH
        )
    table[count:, :] = jnp.zeros((table.shape[0] - count, units), jnp.float32)

    def widen(s, carry):
        fetch(s).wait()
        table[pl.ds(pl.multiple_of(s * step, step), step), :] = land[s % 4].astype(jnp.float32)

        @pl.when(s + 4 < steps)
        def _():
            fetch(s + 4).start()

        return carry

    lax.fori_loop(0, steps, widen, 0)
    pl.semaphore_wait(barrier, hid - 1)
    bias = bias_ref[...]

    def target(d):
        chip = (me // 2 + d // 2 + 1) % chips
        return chip * 2 + (me % 2 + 1 + d) % 2

    def send(dest, c):
        return pltpu.make_async_remote_copy(
            src_ref=act.at[pl.ds(pl.multiple_of(dest * share + c * part, part), part), :],
            dst_ref=got.at[me, pl.ds(pl.multiple_of(c * part, part), part), :],
            send_sem=send_sem.at[dest, c],
            recv_sem=recv_sem.at[me, c],
            device_id={"hid": dest},
            device_id_type=pl.DeviceIdType.MESH,
        )

    def block(n, carry):
        dest, c = target(n // PARTS), n % PARTS
        first = dest * share + c * part

        def some(i, carry):
            base = first + i * TILE
            for j in range(TILE):
                p = base + j
                row = table[pl.ds(idx_ref[p], 1), :] + table[pl.ds(idx_ref[prods + p], 1), :]
                group[pl.ds(j, 1), :] = row + table[pl.ds(idx_ref[2 * prods + p], 1), :]
            act[pl.ds(pl.multiple_of(base, TILE), TILE), :] = gelu_tanh(group[...] + bias).astype(
                jnp.bfloat16
            )
            return carry

        lax.fori_loop(0, part // TILE, some, 0)

        @pl.when(dest != me)
        def _():
            send(dest, c).start()

        return carry

    lax.fori_loop(0, hid * PARTS, block, 0)

    def weights(source):
        return w_ref[pl.ds(pl.multiple_of(source * units, units), units), :]

    mine = act[pl.ds(pl.multiple_of(me * share, share), share), :]
    total[...] = jnp.dot(mine, weights(me), preferred_element_type=jnp.float32)

    def add(d, carry):
        source = target((d + hid - 2) % hid)
        for c in range(PARTS):
            pltpu.make_async_copy(
                got.at[source, pl.ds(c * part, part), :],
                got.at[source, pl.ds(c * part, part), :],
                recv_sem.at[source, c],
            ).wait()
        total[...] += jnp.dot(got[source], weights(source), preferred_element_type=jnp.float32)
        return carry

    add(0, 0)
    lax.fori_loop(2, hid, add, 0)
    last = gelu_tanh(total[...] + b_ref[...]) * out_w_ref[...]
    score_ref[...] = jnp.sum(last, axis=1, keepdims=True)

    def done(n, carry):
        send(target(n // PARTS), n % PARTS).wait_send()
        return carry

    lax.fori_loop(0, (hid - 1) * PARTS, done, 0)


def pick(hid, idx, piece, bias, w_second, b_second, w_third):
    prods = idx.shape[0] // 3
    count, units = piece.shape
    wide = w_second.shape[1]
    share = prods // hid
    step = min(512, count // 4)
    return pl.pallas_call(
        functools.partial(pick_kernel, hid),
        out_shape=jax.ShapeDtypeStruct((share, 1), jnp.float32),
        in_specs=[
            pl.BlockSpec(memory_space=pltpu.SMEM),
            pl.BlockSpec(memory_space=pl.ANY),
        ]
        + [pl.BlockSpec(memory_space=pltpu.VMEM)] * 4,
        out_specs=pl.BlockSpec(memory_space=pltpu.VMEM),
        scratch_shapes=[
            pltpu.VMEM((count + 8, units), jnp.float32),
            pltpu.VMEM((4, step, units), jnp.bfloat16),
            pltpu.VMEM((TILE, units), jnp.float32),
            pltpu.VMEM((prods, units), jnp.bfloat16),
            pltpu.VMEM((hid, share, units), jnp.bfloat16),
            pltpu.VMEM((share, wide), jnp.float32),
            pltpu.SemaphoreType.DMA((4,)),
            pltpu.SemaphoreType.DMA((hid, PARTS)),
            pltpu.SemaphoreType.DMA((hid, PARTS)),
        ],
        compiler_params=pltpu.CompilerParams(
            collective_id=1, has_side_effects=True, vmem_limit_bytes=48 << 20
        ),
    )(idx, piece, bias, w_second, b_second, w_third)


def local(
    prod, hid, fingerprints, w_first, b_first, w_second, b_second, w_third, synth_block, synth_row, third_used
):
    syn_rows = fingerprints.shape[0]
    piece = spread(fingerprints, w_first, prod)
    glob = synth_block * syn_rows + synth_row
    third = jnp.where(third_used > 0, glob[:, 2], syn_rows * prod)
    idx = jnp.concatenate([glob[:, 0], glob[:, 1], third])
    score = pick(
        hid, idx, piece, b_first[None, :], w_second, b_second[None, :], w_third[None, :]
    )
    return score.reshape(-1)


def solution(mesh):
    placed = (
        P("prod", None),
        P(None, "hid"),
        P("hid"),
        P(),
        P(),
        P(),
        P("prod", None),
        P("prod", None),
        P("prod"),
    )
    return jax.shard_map(
        functools.partial(local, mesh.shape["prod"], mesh.shape["hid"]),
        mesh=mesh,
        in_specs=placed,
        out_specs=P(("prod", "hid")),
        check_vma=False,
    )
```

```python
import functools

import jax
import jax.numpy as jnp
from jax import lax
from jax.experimental import pallas as pl
from jax.experimental.pallas import tpu as pltpu
from jax.sharding import PartitionSpec as P

CHUNKS = 4
SLICES = 8
BUFFERS = 8
TILE = 16
PARTS = 4


def gelu_tanh(value):
    return (
        0.5
        * value
        * (1.0 + jnp.tanh(0.7978845608028654 * (value + 0.044715 * value * value * value)))
    )


def offsets(size):
    out = [(0, 0)]
    for far in range(1, size):
        out += [(far, far), (far, -far)]
    return out


def spread_kernel(nz, ny, fp_ref, w_ref, out_ref, w_all, fp_buf, acc, own, w_sem, fp_sem, own_sem, send_sem, recv_sem):
    me = lax.axis_index("prod")
    z, y = me // ny, me % ny
    rows = own.shape[0]
    step = rows // CHUNKS
    depth = w_ref.shape[0] // SLICES
    total = CHUNKS * SLICES

    def w_copy(k):
        part = pl.ds(pl.multiple_of(k * depth, depth), depth)
        return pltpu.make_async_copy(w_ref.at[part, :], w_all.at[part, :], w_sem.at[k])

    def fp_copy(s):
        slot = s % BUFFERS
        return pltpu.make_async_copy(
            fp_ref.at[
                pl.ds(pl.multiple_of((s // SLICES) * step, step), step),
                pl.ds(pl.multiple_of((s % SLICES) * depth, depth), depth),
            ],
            fp_buf.at[slot],
            fp_sem.at[slot],
        )

    for k in range(SLICES):
        w_copy(k).start()
        fp_copy(k).start()

    ways = (
        (z + 1 < nz, me + ny),
        (z >= 1, me - ny),
        (y + 1 < ny, me + 1),
        (y >= 1, me - 1),
    )
    barrier = pltpu.get_barrier_semaphore()
    count = jnp.int32(0)
    for there, target in ways:
        count = count + there.astype(jnp.int32)

        @pl.when(there)
        def _():
            pl.semaphore_signal(
                barrier, inc=1, device_id={"prod": target}, device_id_type=pl.DeviceIdType.MESH
            )

    pl.semaphore_wait(barrier, count)

    def place(src, c):
        return pl.ds(pl.multiple_of(src * rows + c * step, step), step)

    second = step * 3 // 256 * 16
    spans = ((0, step - second), (step - second, second))

    def piece_of(start, way):
        skip, size = spans[way]
        return pl.ds(pl.multiple_of(start + skip, 16), size)

    def arrived(src, c, order):
        there = out_ref.at[piece_of(src * rows + c * step, order), :]
        pltpu.make_async_copy(there, there, recv_sem.at[src, c * 2 + order]).wait()

    def send(c, zs, ys, mine, act):
        send_part(c, zs, ys, mine, act, 0)
        send_part(c, zs, ys, mine, act, 1)

    def send_part(c, zs, ys, mine, act, order):
        src = zs * ny + ys
        in_col, in_row = y == ys, z == zs
        go_z = in_col if order == 0 else (z >= 0)
        go_y = in_row if order == 1 else (y >= 0)
        want = (
            jnp.logical_and(go_z, z >= zs),
            jnp.logical_and(go_z, z <= zs),
            jnp.logical_and(go_y, y >= ys),
            jnp.logical_and(go_y, y <= ys),
        )
        for way, ((there, target), wish) in enumerate(zip(ways, want)):

            @pl.when(jnp.logical_and(there, wish))
            def _():
                source = (
                    own.at[piece_of(c * step, order), :]
                    if mine
                    else out_ref.at[piece_of(src * rows + c * step, order), :]
                )
                copy = pltpu.make_async_remote_copy(
                    src_ref=source,
                    dst_ref=out_ref.at[piece_of(src * rows + c * step, order), :],
                    send_sem=send_sem.at[way, src, c * 2 + order],
                    recv_sem=recv_sem.at[src, c * 2 + order],
                    device_id={"prod": target},
                    device_id_type=pl.DeviceIdType.MESH,
                )
                if act:
                    copy.start()
                else:
                    copy.wait_send()

    def keep(t):
        part = pl.ds(pl.multiple_of(t * step, step), step)
        return pltpu.make_async_copy(own.at[part, :], out_ref.at[place(me, t), :], own_sem.at[t])

    def compute(t, carry):
        def one(k, carry):
            s = t * SLICES + k

            @pl.when(t == 0)
            def _():
                w_copy(k).wait()

            fp_copy(s).wait()
            part = pl.ds(pl.multiple_of(k * depth, depth), depth)
            term = jnp.dot(fp_buf[s % BUFFERS], w_all[part, :], preferred_element_type=jnp.float32)

            @pl.when(k == 0)
            def _():
                acc[...] = term

            @pl.when(k > 0)
            def _():
                acc[...] += term

            @pl.when(s + BUFFERS < total)
            def _():
                fp_copy(s + BUFFERS).start()

            return carry

        lax.fori_loop(0, SLICES, one, 0)
        own[pl.ds(pl.multiple_of(t * step, step), step), :] = acc[...].astype(jnp.bfloat16)
        send(t, z, y, True, True)
        keep(t).start()
        return carry

    apart = [
        (dz, dy, far_z + far_y)
        for (far_z, dz) in offsets(nz)
        for (far_y, dy) in offsets(ny)
        if far_z + far_y > 0
    ]
    apart.sort(key=lambda item: item[2])
    furthest = apart[-1][2]

    def visit(c, act, dz, dy):
        zs, ys = z + dz, y + dy
        inside = (zs >= 0) & (zs < nz) & (ys >= 0) & (ys < ny) & (c >= 0) & (c < CHUNKS)

        @pl.when(inside)
        def _():
            for order in range(2):
                if act:
                    arrived(zs * ny + ys, c, order)
                send_part(c, zs, ys, False, act, order)

    def turn(r, carry):
        for dz, dy, far in apart:
            visit(r - (far - 1), True, dz, dy)
        return carry

    lax.fori_loop(0, 2, compute, 0)
    turn(0, 0)
    lax.fori_loop(2, CHUNKS, compute, 0)
    lax.fori_loop(1, CHUNKS + furthest - 1, turn, 0)

    def finish(c, carry):
        send(c, z, y, True, False)
        keep(c).wait()
        for dz, dy, _ in apart:
            visit(c, False, dz, dy)
        return carry

    lax.fori_loop(0, CHUNKS, finish, 0)


def spread(fingerprints, w_first, prod):
    rows, depth = fingerprints.shape
    units = w_first.shape[1]
    nz = 4 if prod % 4 == 0 else 1
    ny = prod // nz
    return pl.pallas_call(
        functools.partial(spread_kernel, nz, ny),
        out_shape=jax.ShapeDtypeStruct((rows * prod, units), jnp.bfloat16),
        in_specs=[pl.BlockSpec(memory_space=pl.ANY)] * 2,
        out_specs=pl.BlockSpec(memory_space=pl.ANY),
        scratch_shapes=[
            pltpu.VMEM((depth, units), jnp.bfloat16),
            pltpu.VMEM((BUFFERS, rows // CHUNKS, depth // SLICES), jnp.bfloat16),
            pltpu.VMEM((rows // CHUNKS, units), jnp.float32),
            pltpu.VMEM((rows, units), jnp.bfloat16),
            pltpu.SemaphoreType.DMA((SLICES,)),
            pltpu.SemaphoreType.DMA((BUFFERS,)),
            pltpu.SemaphoreType.DMA((CHUNKS,)),
            pltpu.SemaphoreType.DMA((4, prod, CHUNKS * 2)),
            pltpu.SemaphoreType.DMA((prod, CHUNKS * 2)),
        ],
        compiler_params=pltpu.CompilerParams(
            collective_id=0, has_side_effects=True, vmem_limit_bytes=48 << 20
        ),
        cost_estimate=pl.CostEstimate(
            flops=2 * rows * depth * units,
            bytes_accessed=2 * (rows * depth + depth * units + rows * prod * units),
            transcendentals=0,
        ),
    )(fingerprints, w_first)


def pick_kernel(
    hid, idx_ref, piece_ref, bias_ref, w_ref, b_ref, out_w_ref, score_ref, table, land, group, act, got, total, sem, send_sem, recv_sem
):
    me = lax.axis_index("hid")
    chips = hid // 2
    count = piece_ref.shape[0]
    step = land.shape[1]
    prods, units = act.shape
    share = prods // hid
    part = share // PARTS
    steps = count // step

    def fetch(s):
        return pltpu.make_async_copy(
            piece_ref.at[pl.ds(pl.multiple_of(s * step, step), step), :],
            land.at[s % 4],
            sem.at[s % 4],
        )

    for s in range(4):
        fetch(s).start()
    barrier = pltpu.get_barrier_semaphore()
    for j in range(1, hid):
        pl.semaphore_signal(
            barrier, inc=1, device_id={"hid": (me + j) % hid}, device_id_type=pl.DeviceIdType.MESH
        )
    table[count:, :] = jnp.zeros((table.shape[0] - count, units), jnp.float32)

    def widen(s, carry):
        fetch(s).wait()
        table[pl.ds(pl.multiple_of(s * step, step), step), :] = land[s % 4].astype(jnp.float32)

        @pl.when(s + 4 < steps)
        def _():
            fetch(s + 4).start()

        return carry

    lax.fori_loop(0, steps, widen, 0)
    pl.semaphore_wait(barrier, hid - 1)
    bias = bias_ref[...]

    def target(d):
        chip = (me // 2 + d // 2 + 1) % chips
        return chip * 2 + (me % 2 + 1 + d) % 2

    def send(dest, c):
        return pltpu.make_async_remote_copy(
            src_ref=act.at[pl.ds(pl.multiple_of(dest * share + c * part, part), part), :],
            dst_ref=got.at[me, pl.ds(pl.multiple_of(c * part, part), part), :],
            send_sem=send_sem.at[dest, c],
            recv_sem=recv_sem.at[me, c],
            device_id={"hid": dest},
            device_id_type=pl.DeviceIdType.MESH,
        )

    def block(n, carry):
        dest, c = target(n // PARTS), n % PARTS
        first = dest * share + c * part

        def some(i, carry):
            base = first + i * TILE
            for j in range(TILE):
                p = base + j
                row = table[pl.ds(idx_ref[p], 1), :] + table[pl.ds(idx_ref[prods + p], 1), :]
                group[pl.ds(j, 1), :] = row + table[pl.ds(idx_ref[2 * prods + p], 1), :]
            act[pl.ds(pl.multiple_of(base, TILE), TILE), :] = gelu_tanh(group[...] + bias).astype(
                jnp.bfloat16
            )
            return carry

        lax.fori_loop(0, part // TILE, some, 0)

        @pl.when(dest != me)
        def _():
            send(dest, c).start()

        return carry

    lax.fori_loop(0, hid * PARTS, block, 0)

    def weights(source):
        return w_ref[pl.ds(pl.multiple_of(source * units, units), units), :]

    mine = act[pl.ds(pl.multiple_of(me * share, share), share), :]
    total[...] = jnp.dot(mine, weights(me), preferred_element_type=jnp.float32)

    def add(d, carry):
        source = target((d + hid - 2) % hid)
        for c in range(PARTS):
            pltpu.make_async_copy(
                got.at[source, pl.ds(c * part, part), :],
                got.at[source, pl.ds(c * part, part), :],
                recv_sem.at[source, c],
            ).wait()
        total[...] += jnp.dot(got[source], weights(source), preferred_element_type=jnp.float32)
        return carry

    add(0, 0)
    lax.fori_loop(2, hid, add, 0)
    last = gelu_tanh(total[...] + b_ref[...]) * out_w_ref[...]
    score_ref[...] = jnp.sum(last, axis=1, keepdims=True)

    def done(n, carry):
        send(target(n // PARTS), n % PARTS).wait_send()
        return carry

    lax.fori_loop(0, (hid - 1) * PARTS, done, 0)


def pick(hid, idx, piece, bias, w_second, b_second, w_third):
    prods = idx.shape[0] // 3
    count, units = piece.shape
    wide = w_second.shape[1]
    share = prods // hid
    step = min(512, count // 4)
    return pl.pallas_call(
        functools.partial(pick_kernel, hid),
        out_shape=jax.ShapeDtypeStruct((share, 1), jnp.float32),
        in_specs=[
            pl.BlockSpec(memory_space=pltpu.SMEM),
            pl.BlockSpec(memory_space=pl.ANY),
        ]
        + [pl.BlockSpec(memory_space=pltpu.VMEM)] * 4,
        out_specs=pl.BlockSpec(memory_space=pltpu.VMEM),
        scratch_shapes=[
            pltpu.VMEM((count + 8, units), jnp.float32),
            pltpu.VMEM((4, step, units), jnp.bfloat16),
            pltpu.VMEM((TILE, units), jnp.float32),
            pltpu.VMEM((prods, units), jnp.bfloat16),
            pltpu.VMEM((hid, share, units), jnp.bfloat16),
            pltpu.VMEM((share, wide), jnp.float32),
            pltpu.SemaphoreType.DMA((4,)),
            pltpu.SemaphoreType.DMA((hid, PARTS)),
            pltpu.SemaphoreType.DMA((hid, PARTS)),
        ],
        compiler_params=pltpu.CompilerParams(
            collective_id=1, has_side_effects=True, vmem_limit_bytes=48 << 20
        ),
    )(idx, piece, bias, w_second, b_second, w_third)


def local(
    prod, hid, fingerprints, w_first, b_first, w_second, b_second, w_third, synth_block, synth_row, third_used
):
    syn_rows = fingerprints.shape[0]
    piece = spread(fingerprints, w_first, prod)
    glob = synth_block * syn_rows + synth_row
    third = jnp.where(third_used > 0, glob[:, 2], syn_rows * prod)
    idx = jnp.concatenate([glob[:, 0], glob[:, 1], third])
    score = pick(
        hid, idx, piece, b_first[None, :], w_second, b_second[None, :], w_third[None, :]
    )
    return score.reshape(-1)


def solution(mesh):
    placed = (
        P("prod", None),
        P(None, "hid"),
        P("hid"),
        P(),
        P(),
        P(),
        P("prod", None),
        P("prod", None),
        P("prod"),
    )
    return jax.shard_map(
        functools.partial(local, mesh.shape["prod"], mesh.shape["hid"]),
        mesh=mesh,
        in_specs=placed,
        out_specs=P(("prod", "hid")),
        check_vma=False,
    )
```
